256 devices in a mesh: seq: 8 (over z), tp: 8 (over y_hi, x), rep: 4 (over y_lo, core).
Axes of the slice: x: 4, y: 4 (y_hi: 2, y_lo: 2; y = y_hi * 2 + y_lo), z: 8, core: 2. Of those that a mesh axis runs over, the one named last changes fastest.
Arguments:
- query_span: bfloat16 [4096, 8192], P(('seq', 'rep'), 'tp'), may hold values from -20 to 20
- key_span: bfloat16 [4096, 1024], P(('seq', 'rep'), 'tp'), may hold values from -5 to 5
- value_span: bfloat16 [4096, 1024], P(('seq', 'rep'), 'tp'), may hold values from -5 to 5
- context_keys: bfloat16 [16384, 1024], P(('seq', 'rep'), 'tp'), may hold values from -4 to 4
- context_values: bfloat16 [16384, 1024], P(('seq', 'rep'), 'tp'), may hold values from -5 to 5
- span_offset: int32 [1], replicated, may hold values from 8192 to 16384
- decode_query: bfloat16 [8, 128, 2048], P('tp', ('seq', 'rep')), may hold values from -20 to 20
- lengths: int32 [2, 128], P(None, ('seq', 'rep')), may hold values from 128 to 512, as said below
- slot_table: int32 [2, 128], P(None, ('seq', 'rep')), may hold values from 0 to 5, as said below
- cache_keys: bfloat16 [8, 192, 512, 256], P('tp', ('seq', 'rep')), may hold values from -4 to 4
- cache_values: bfloat16 [8, 192, 512, 256], P('tp', ('seq', 'rep')), may hold values from -5 to 5
Outputs:
- attended: bfloat16 [4096, 8192], P(('seq', 'rep'), 'tp')
- handed: bfloat16 [8, 2048, 512], P('tp', ('seq', 'rep'))
- decoded: bfloat16 [8, 128, 2048], P('tp', ('seq', 'rep'))
The draws below stay inside these ranges and needn't reach their ends.
Inputs may be any that keep to these rules, and one draw needn't show every extreme that they name: `lengths`: some request has exactly 512 cached positions and some has 128. `slot_table`: the 4 requests of one half in one block of 4 requests have distinct slots.
All inputs are finite; a program needn't handle non-finite values.
Results may differ from the reference program's by a relative error of at most 0.007.
Values may be sent and summed in bfloat16 or wider, within the bound.
A program may use at most 64 MiB of HBM per device.

```python
import jax
import jax.numpy as jnp
from jax import lax

H = 64
KVH = 8
HD = 128
QD = 128
REQ_DEV = 4
CACHE_LEN = 512
SLOTS_DEV = 6
SPAN = 4096
CTX = 16384
REQS = 128
SLOTS = 192
PAIR_COLS = 256
N_TP = 8


def draw_query_span(key, part):
    key = jax.random.fold_in(key, 101)
    draw_base = jnp.clip(3.0 * jax.random.normal(key, (SPAN, H * HD), jnp.float32), -12.0, 12.0)
    return draw_base.astype(jnp.bfloat16)


def draw_context_keys(key, part):
    key = jax.random.fold_in(key, 102)
    draw_base = jnp.clip(jax.random.normal(key, (CTX, KVH * HD), jnp.float32), -4.0, 4.0)
    return draw_base.astype(jnp.bfloat16)


def draw_decode_query(key, part):
    key = jax.random.fold_in(key, 105)
    columns = 2 * (H // N_TP) * HD
    draw_base = jnp.clip(3.0 * jax.random.normal(key, (N_TP, REQS, columns), jnp.float32), -12.0, 12.0)
    return draw_base.astype(jnp.bfloat16)


def draw_cache_keys(key, part):
    pair_heads = 2 * (KVH // N_TP)
    key = jax.random.fold_in(key, 106)
    shape_all = (N_TP, SLOTS, CACHE_LEN, pair_heads * HD)
    draw_base = jnp.clip(jax.random.normal(key, shape_all, jnp.float32), -4.0, 4.0)
    return draw_base.astype(jnp.bfloat16)


def draw_lengths(key, part):
    key = jax.random.fold_in(key, 103)
    key_live, key_long, key_short = jax.random.split(key, 3)
    live_len = jax.random.randint(key_live, (2 * REQS,), CACHE_LEN // 4, CACHE_LEN + 1)
    longest = jax.random.randint(key_long, (), 0, 2 * REQS)
    shortest = (longest + 1 + jax.random.randint(key_short, (), 0, 2 * REQS - 1)) % (2 * REQS)
    request_ids = jnp.arange(2 * REQS)
    live_len = jnp.where(request_ids == longest, CACHE_LEN, live_len)
    live_len = jnp.where(request_ids == shortest, CACHE_LEN // 4, live_len)
    return live_len.reshape(2, REQS).astype(jnp.int32)


def draw_slot_table(key, part):
    key = jax.random.fold_in(key, 104)
    blocks_all = 2 * (REQS // REQ_DEV)
    key_perm, key_high, key_low = jax.random.split(key, 3)

    def one_order(sub_key):
        return jax.random.permutation(sub_key, SLOTS_DEV)
    orders = jax.vmap(one_order)(jax.random.split(key_perm, blocks_all))
    high_block = jax.random.randint(key_high, (), 0, blocks_all)
    low_block = (high_block + 1 + jax.random.randint(key_low, (), 0, blocks_all - 1)) % blocks_all
    shift_high = jnp.argmax(orders == SLOTS_DEV - 1, axis=1)
    shift_low = jnp.argmax(orders == 0, axis=1)
    block_ids = jnp.arange(blocks_all)
    shifts = jnp.where(block_ids == high_block, shift_high, jnp.where(block_ids == low_block, shift_low, 0))
    columns = (jnp.arange(SLOTS_DEV)[None, :] + shifts[:, None]) % SLOTS_DEV
    rolled = jnp.take_along_axis(orders, columns, axis=1)
    return rolled[:, :REQ_DEV].reshape(2, REQS).astype(jnp.int32)


def block_scale(stream_key, extent, cuts, low, largest):
    level = 1.0
    for dim, parts in cuts:
        draws = jax.random.uniform(jax.random.fold_in(jax.random.fold_in(stream_key, 6), dim), (parts,), jnp.float32, low / len(cuts), largest / len(cuts))
        level = level * jnp.repeat(jnp.exp(draws), extent[dim] // parts).reshape((-1,) + (1,) * (len(extent) - 1 - dim))
    return level


def normal_values(key, shape, width, bound, shards=(), held_as=jnp.bfloat16):
    level = block_scale(key, shape, shards, -0.22, 0.18) if shards else 1.0
    values = jax.random.normal(key, shape, jnp.float32) * width * level
    return jnp.minimum(jnp.maximum(values, -bound), bound).astype(held_as)


def setup_inputs(seed: int = 0) -> dict:
    keys = jax.random.split(jax.random.key(seed), 12)
    return {
        "query_span": draw_query_span(jax.random.fold_in(keys[11], 71), 0),
        "key_span": normal_values(keys[1], (SPAN, KVH * HD), 1.0, 5.0, ((0, 32), (1, 8))),
        "value_span": normal_values(keys[2], (SPAN, KVH * HD), 1.0, 5.0, ((0, 32), (1, 8))),
        "context_keys": draw_context_keys(jax.random.fold_in(keys[11], 71), 0),
        "context_values": normal_values(keys[4], (CTX, KVH * HD), 1.0, 5.0, ((0, 32), (1, 8))),
        "span_offset": jax.random.randint(keys[5], (1,), CTX // 2, CTX + 1).astype(jnp.int32),
        "decode_query": draw_decode_query(jax.random.fold_in(keys[11], 71), 0),
        "lengths": draw_lengths(jax.random.fold_in(keys[11], 71), 0),
        "slot_table": draw_slot_table(jax.random.fold_in(keys[11], 71), 0),
        "cache_keys": draw_cache_keys(jax.random.fold_in(keys[11], 71), 0),
        "cache_values": normal_values(keys[10], (N_TP, SLOTS, CACHE_LEN, PAIR_COLS), 1.0, 5.0, ((0, 8), (1, 32))),
    }


def prefill_rows(block_index, query_span, key_rows, value_rows, valid_limit, score_scale):
    groups = H // KVH
    row_block = lax.dynamic_slice_in_dim(query_span, block_index * QD, QD, 0).astype(jnp.float32)
    row_block = row_block.reshape(QD, KVH, groups, HD)
    row_ids = block_index * QD + jnp.arange(QD, dtype=jnp.int32)
    key_ids = jnp.arange(CTX + SPAN, dtype=jnp.int32)
    is_valid = jnp.where(key_ids[None, :] < CTX, key_ids[None, :] < valid_limit, key_ids[None, :] - CTX <= row_ids[:, None])

    def head_mix(head_index):
        query_head = lax.dynamic_index_in_dim(row_block, head_index, 1, keepdims=False)
        key_head = lax.dynamic_index_in_dim(key_rows, head_index, 1, keepdims=False)
        value_head = lax.dynamic_index_in_dim(value_rows, head_index, 1, keepdims=False)
        scores = jnp.einsum("qgd,nd->qgn", query_head, key_head) * score_scale
        row_max = jnp.max(jnp.where(is_valid[:, None, :], scores, -jnp.inf), axis=-1)
        weights = jnp.where(is_valid[:, None, :], jnp.exp(scores - row_max[..., None]), 0.0)
        weight_sum = jnp.sum(weights, axis=-1)
        rounded = lax.optimization_barrier(weights.astype(jnp.bfloat16)).astype(jnp.float32)
        return jnp.einsum("qgn,nd->qgd", rounded, value_head) / weight_sum[..., None]

    mixed_heads = lax.map(head_mix, jnp.arange(KVH, dtype=jnp.int32))
    return jnp.transpose(mixed_heads, (1, 0, 2, 3)).reshape(QD, H * HD).astype(jnp.bfloat16)


def handover_layout(key_span, value_span):
    half_count = N_TP // 2
    per_dev = KVH // N_TP
    blocks_all = SPAN // QD
    key_split = key_span.reshape(blocks_all, 2, QD // 2, KVH * HD)
    value_split = value_span.reshape(blocks_all, 2, QD // 2, KVH * HD)
    outputs = []
    for device in range(N_TP):
        half_index = device // half_count
        key_half = key_split[:, half_index].reshape(SPAN // 2, KVH * HD)
        value_half = value_split[:, half_index].reshape(SPAN // 2, KVH * HD)
        pieces = []
        for source in (device % half_count, device % half_count + half_count):
            low_col = source * per_dev * HD
            high_col = low_col + per_dev * HD
            pieces.append(key_half[:, low_col:high_col])
            pieces.append(value_half[:, low_col:high_col])
        outputs.append(jnp.concatenate(pieces, axis=1))
    return jnp.stack(outputs, axis=0)


def decode_device(device, decode_query, lengths, slot_table, cache_keys, cache_values, score_scale):
    half_index = device // (N_TP // 2)
    live_len = lax.dynamic_index_in_dim(lengths, half_index, 0, keepdims=False)
    slot_picks = lax.dynamic_index_in_dim(slot_table, half_index, 0, keepdims=False)
    blocks = jnp.arange(REQS, dtype=jnp.int32) // REQ_DEV
    slot_rows = (blocks * SLOTS_DEV + slot_picks).astype(jnp.int32)
    pair_heads = 2 * (KVH // N_TP)
    groups = H // KVH
    key_cache = lax.dynamic_index_in_dim(cache_keys, device, 0, keepdims=False)
    value_cache = lax.dynamic_index_in_dim(cache_values, device, 0, keepdims=False)
    key_rows = jnp.take(key_cache, slot_rows, axis=0).astype(jnp.float32).reshape(REQS, CACHE_LEN, pair_heads, HD)
    value_rows = jnp.take(value_cache, slot_rows, axis=0).astype(jnp.float32).reshape(REQS, CACHE_LEN, pair_heads, HD)
    queries = lax.dynamic_index_in_dim(decode_query, device, 0, keepdims=False).astype(jnp.float32)
    queries = queries.reshape(REQS, pair_heads, groups, HD)
    scores = jnp.einsum("bhgd,blhd->bhgl", queries, key_rows) * score_scale
    is_valid = (jnp.arange(CACHE_LEN, dtype=jnp.int32)[None, :] < live_len[:, None])[:, None, None, :]
    row_max = jnp.max(jnp.where(is_valid, scores, -jnp.inf), axis=-1)
    weights = jnp.where(is_valid, jnp.exp(scores - row_max[..., None]), 0.0)
    weight_sum = jnp.sum(weights, axis=-1)
    rounded = lax.optimization_barrier(weights.astype(jnp.bfloat16)).astype(jnp.float32)
    mixed_out = jnp.einsum("bhgl,blhd->bhgd", rounded, value_rows) / weight_sum[..., None]
    return mixed_out.reshape(REQS, 2 * (H // N_TP) * HD).astype(jnp.bfloat16)


def reference(query_span, key_span, value_span, context_keys, context_values, span_offset, decode_query, lengths, slot_table, cache_keys, cache_values):
    score_scale = 1.0 / (HD ** 0.5)
    key_rows = jnp.concatenate([context_keys, key_span], axis=0).astype(jnp.float32).reshape(CTX + SPAN, KVH, HD)
    value_rows = jnp.concatenate([context_values, value_span], axis=0).astype(jnp.float32).reshape(CTX + SPAN, KVH, HD)
    valid_limit = span_offset[0]

    def one_block(block_index):
        return prefill_rows(block_index, query_span, key_rows, value_rows, valid_limit, score_scale)

    attended = lax.map(one_block, jnp.arange(SPAN // QD, dtype=jnp.int32)).reshape(SPAN, H * HD)
    handed = handover_layout(key_span, value_span)

    def one_device(device):
        return decode_device(device, decode_query, lengths, slot_table, cache_keys, cache_values, score_scale)

    decoded = lax.map(one_device, jnp.arange(N_TP, dtype=jnp.int32))
    return attended, handed, decoded
```

```python
import jax
import jax.numpy as jnp
from jax import lax
from jax.experimental import pallas as pl
from jax.experimental.pallas import tpu as pltpu
from jax.sharding import PartitionSpec as P

HD = 128
GROUPS = 8
QROWS = 128
CROWS = 512
Z = 8
SCALE2 = 1.4426950408889634 / 128**0.5
MASKED = -1e31
M_START = -1e29
SPAN_BASE = 7168
LAST_BASE = 9216
ALL_ROWS = 10240
TILE = 256
MESH = pl.DeviceIdType.MESH
BF = jnp.bfloat16
F32 = jnp.float32

CK, CV, SK, SV = range(4)
SLOT_OF = ((0, 1, 3, 5, 7), (0, 2, 4, 6, 7))

STEPS = (
    (0, 0, 1024),
    (1, 0, 1024),
    (1, 1024, 2048),
    (0, 1024, 2048),
    (1, SPAN_BASE, 2048),
    (0, SPAN_BASE, 2048),
    (1, 3072, 2048),
    (0, 3072, 2048),
    (1, 5120, 2048),
    (1, LAST_BASE, 1024),
    (0, 5120, 2048),
    (0, LAST_BASE, 1024),
)
SEND_AFTER = 9


def pick(i, table):
    total = jnp.int32(0)
    for at, value in enumerate(table):
        if value:
            total = total + jnp.where(i == at, jnp.int32(value), jnp.int32(0))
    return total


def kernel(
    query,
    key_span,
    value_span,
    ctx_k,
    ctx_v,
    offset,
    dec_q,
    lengths,
    slots,
    cache_k,
    cache_v,
    out_att,
    out_hand,
    out_dec,
    qb,
    kall,
    vall,
    mask,
    ident,
    m_ref,
    acc_ref,
    o_send,
    o_recv,
    l_send,
    l_recv,
    hbuf,
    dqb,
    ckb,
    cvb,
    ring_send,
    ring_recv,
    core_send,
    core_recv,
    misc_send,
    misc_recv,
    local_sem,
):
    z = lax.axis_index("seq")
    tp = lax.axis_index("tp")
    rep = lax.axis_index("rep")
    y = rep // 2
    c = rep % 2
    half = tp // 4
    nxt = {"seq": (z + 1) % Z}
    prv = {"seq": (z + Z - 1) % Z}
    core = {"rep": y * 2 + (1 - c)}
    other = {"rep": (1 - y) * 2 + c}
    mate = {"tp": (1 - half) * 4 + tp % 4}

    def rows(slot, kind, which):
        if kind in (CK, CV):
            base = slot * 1024 if slot < 7 else LAST_BASE
            return pl.ds(pl.multiple_of(base + which * CROWS, CROWS), CROWS)
        return pl.ds(pl.multiple_of(SPAN_BASE + slot * 256 + which * QROWS, QROWS), QROWS)

    def held(slot, kind, which):
        ref = kall if kind in (CK, SK) else vall
        return ref.at[rows(slot, kind, which), :]

    own = (ctx_k, ctx_v, key_span, value_span)

    def ring(way, hop, kind):
        src = own[kind] if hop == 1 else held(SLOT_OF[way][hop - 1], kind, c)
        at = (way * 4 + hop - 1) * 4 + kind
        return pltpu.make_async_remote_copy(
            src_ref=src,
            dst_ref=held(SLOT_OF[way][hop], kind, c),
            send_sem=ring_send.at[at],
            recv_sem=ring_recv.at[at],
            device_id=nxt if way == 0 else prv,
            device_id_type=MESH,
        )

    def has_hop(way, hop, kind):
        return hop <= 3 or (hop == 4 and (kind in (CK, SK)) == (way == 0))

    def across(slot, kind, incoming=False):
        at = slot * 4 + kind
        return pltpu.make_async_remote_copy(
            src_ref=own[kind] if slot == 0 else held(slot, kind, c),
            dst_ref=held(slot, kind, 1 - c if incoming else c),
            send_sem=core_send.at[at],
            recv_sem=core_recv.at[at],
            device_id=core,
            device_id_type=MESH,
        )

    def pass_on(hop, kind):
        for way in (0, 1):
            if has_hop(way, hop, kind):
                ring(way, hop, kind).wait_recv()
                if has_hop(way, hop + 1, kind):
                    ring(way, hop + 1, kind).start()
                across(SLOT_OF[way][hop], kind).start()

    def from_core(slot_list, kinds):
        for slot in slot_list:
            for kind in kinds:
                across(slot, kind, True).wait_recv()

    def misc(at, src, dst, device):
        return pltpu.make_async_remote_copy(
            src_ref=src,
            dst_ref=dst,
            send_sem=misc_send.at[at],
            recv_sem=misc_recv.at[at],
            device_id=device,
            device_id_type=MESH,
        )

    q_copy = misc(0, query, qb.at[1], other)
    kept = pl.ds(pl.multiple_of(half * 64, 64), 64)
    given = pl.ds(pl.multiple_of((1 - half) * 64, 64), 64)
    hk_copy = misc(1, key_span.at[given, :], hbuf.at[half, 0], mate)
    hv_copy = misc(2, value_span.at[given, :], hbuf.at[half, 1], mate)
    o_copy = misc(3, o_send, o_recv, other)
    l_copy = misc(4, l_send, l_recv, other)

    local = [
        pltpu.make_async_copy(src, dst, local_sem.at[at])
        for at, (src, dst) in enumerate(
            (
                (query, qb.at[0]),
                (ctx_k, held(0, CK, c)),
                (ctx_v, held(0, CV, c)),
                (key_span, held(0, SK, c)),
                (value_span, held(0, SV, c)),
                (dec_q.at[0], dqb),
                (cache_k.at[0], ckb),
                (cache_v.at[0], cvb),
                (key_span.at[kept, :], hbuf.at[half, 0]),
                (value_span.at[kept, :], hbuf.at[half, 1]),
            )
        )
    ]
    barrier = pltpu.get_barrier_semaphore()
    for device in (nxt, prv, core, other, mate):
        pl.semaphore_signal(barrier, inc=1, device_id=device, device_id_type=MESH)
    for copy in local:
        copy.start()
    pl.semaphore_wait(barrier, 5)

    for kind in (SK, SV, CK):
        for way in (0, 1):
            ring(way, 1, kind).start()
    for kind in (CK, CV, SK, SV):
        across(0, kind).start()
    q_copy.start()
    hk_copy.start()
    hv_copy.start()

    row = lax.broadcasted_iota(jnp.int32, (QROWS, HD), 0)
    col = lax.broadcasted_iota(jnp.int32, (QROWS, HD), 1)
    ident[...] = jnp.where(row == col, 1.0, 0.0).astype(BF)
    limit = offset[0]
    long_row = lax.broadcasted_iota(jnp.int32, (CROWS, HD), 0)

    def fill(slot, carry):
        odd = slot % 2
        z_slot = (z + 2 * Z - odd * ((slot + 1) // 2) + (1 - odd) * (slot // 2)) % Z
        for which in (0, 1):
            block = z_slot * 4 + y * 2 + which
            base = slot * 1024 + jnp.where(slot == 7, LAST_BASE - SPAN_BASE, 0) + which * CROWS
            mask[pl.ds(pl.multiple_of(base, CROWS), CROWS), :] = jnp.where(
                long_row + block * CROWS >= limit, MASKED, 0.0
            ).astype(BF)
            for b in (0, 1):
                y_b = y if b == 0 else 1 - y
                ahead = (block - (z * 4 + y_b * 2 + c)) * QROWS
                base = (SPAN_BASE if b == 0 else ALL_ROWS) + slot * 256 + which * QROWS
                mask[pl.ds(pl.multiple_of(base, QROWS), QROWS), :] = jnp.where(
                    row + ahead > col, MASKED, 0.0
                ).astype(BF)
        return carry

    lax.fori_loop(0, 8, fill, 0)
    m_ref[...] = jnp.full_like(m_ref, M_START)
    acc_ref[...] = jnp.zeros_like(acc_ref)

    for kind in (SK, SV):
        pass_on(1, kind)
    for way in (0, 1):
        ring(way, 1, CV).start()

    for copy in local:
        copy.wait()
    dq = dqb[...].astype(F32)
    picked = [slots[half, b] for b in range(4)]
    live = [lengths[half, b] for b in range(4)]
    place = lax.broadcasted_iota(jnp.int32, (64, 512), 1)
    request = lax.broadcasted_iota(jnp.int32, (64, 512), 0) % 8
    ok = jnp.concatenate(
        [(request == b) & (place < live[b]) for b in range(4)], axis=1
    )
    blank = jnp.zeros((4, HD), F32)
    for head in (0, 1):
        lanes = slice(head * HD, (head + 1) * HD)
        q = jnp.concatenate(
            [
                part
                for g in range(GROUPS)
                for part in (dq[:, (head * 8 + g) * HD : (head * 8 + g + 1) * HD], blank)
            ],
            axis=0,
        ).astype(BF)
        k = jnp.concatenate([ckb[picked[b]][:, lanes] for b in range(4)], axis=0)
        v = jnp.concatenate([cvb[picked[b]][:, lanes] for b in range(4)], axis=0)
        s = lax.dot_general(q, k, (((1,), (1,)), ((), ())), preferred_element_type=F32)
        s = jnp.where(ok, s * SCALE2, MASKED)
        top = jnp.max(s, axis=1, keepdims=True)
        w = jnp.where(ok, jnp.exp2(s - top), 0.0)
        total = jnp.sum(w, axis=1, keepdims=True)
        o = lax.dot_general(
            w.astype(BF), v, (((1,), (0,)), ((), ())), preferred_element_type=F32
        )
        o = o / total
        for g in range(GROUPS):
            out_dec[0, :, (head * 8 + g) * HD : (head * 8 + g + 1) * HD] = o[
                g * 8 : g * 8 + 4, :
            ].astype(BF)

    for kind in (SK, SV):
        pass_on(2, kind)

    def scores_block(b, key_off, mask_off, width):
        keys = pl.ds(pl.multiple_of(key_off, 1024), width)
        k = jnp.concatenate(
            [kall[keys, :], mask[pl.ds(pl.multiple_of(mask_off, 1024), width), :]], axis=1
        )
        v = jnp.concatenate([vall[keys, :], jnp.ones((width, HD), BF)], axis=1)
        eye = jnp.concatenate([ident[...]] * 2, axis=0)
        all_s = []
        for t in range(4):
            q = jnp.concatenate(
                [qb[b, :, (2 * t + u) * HD : (2 * t + u + 1) * HD] for u in (0, 1)], axis=0
            )
            q = jnp.concatenate([q, eye], axis=1)
            all_s.append(
                lax.dot_general(q, k, (((1,), (1,)), ((), ())), preferred_element_type=F32)
            )
        for t in range(4):
            s = all_s[t]
            at = pl.ds(t * TILE, TILE)
            before = m_ref[b, at, :]
            now = jnp.maximum(before, jnp.max(s, axis=1, keepdims=True) * SCALE2)
            factor = jnp.exp2(before - now)
            p = jnp.exp2(s * SCALE2 - now[:, :1])
            m_ref[b, at, :] = now
            pv = lax.dot_general(
                p.astype(BF), v, (((1,), (0,)), ((), ())), preferred_element_type=F32
            )
            acc_ref[b, at, :] = acc_ref[b, at, :] * jnp.concatenate([factor, factor], axis=1) + pv

    def duties(step):
        if step == 0:
            from_core((0,), (CK, CV))
        elif step == 1:
            pass_on(3, SK)
            pass_on(3, SV)
            pass_on(1, CK)
            q_copy.wait_recv()
        elif step == 2:
            pass_on(4, SK)
            pass_on(4, SV)
            pass_on(1, CV)
            from_core((1, 2), (CK, CV))
        elif step == 4:
            pass_on(2, CK)
            from_core(range(8), (SK, SV))
        elif step == 5:
            pass_on(2, CV)
        elif step == 6:
            pass_on(3, CK)
            from_core((3, 4), (CK, CV))
        elif step == 7:
            pass_on(3, CV)
        elif step == 8:
            from_core((5, 6), (CK, CV))
        elif step == 9:
            pass_on(4, CK)
            pass_on(4, CV)
            from_core((7,), (CK, CV))

    def one_step(i, carry):
        for step in range(len(STEPS)):
            pl.when(i == step)(lambda step=step: duties(step))
        b = pick(i, [s[0] for s in STEPS])
        off = pick(i, [s[1] for s in STEPS])
        m_off = pick(
            i, [ALL_ROWS if s[0] == 1 and s[1] == SPAN_BASE else s[1] for s in STEPS]
        )
        short = pick(i, [int(s[2] == 1024) for s in STEPS])
        pl.when(short == 1)(lambda: scores_block(b, off, m_off, 1024))
        pl.when(short == 0)(lambda: scores_block(b, off, m_off, 2048))

        @pl.when(i == SEND_AFTER)
        def _():
            eye = ident[...].astype(F32)
            for g in range(GROUPS):
                at = pl.ds(g * QROWS, QROWS)
                total = acc_ref[1, at, HD:]
                o_send[at, :] = (acc_ref[1, at, :HD] / total).astype(BF)
                level = m_ref[1, at, :] + jnp.log(total) * 1.4426950408889634
                l_send[g : g + 1, :] = jnp.sum(level * eye, axis=0, keepdims=True)
            l_copy.start()
            o_copy.start()

        return carry

    lax.fori_loop(0, len(STEPS), one_step, 0)

    hk_copy.wait()
    hv_copy.wait()
    for u in (0, 1):
        for kv in (0, 1):
            out_hand[0, :, (u * 2 + kv) * HD : (u * 2 + kv + 1) * HD] = hbuf[u, kv]
    for way in (0, 1):
        for hop in (1, 2, 3, 4):
            for kind in range(4):
                if has_hop(way, hop, kind):
                    ring(way, hop, kind).wait_send()
    for slot in range(8):
        for kind in range(4):
            across(slot, kind).wait_send()
    q_copy.wait_send()
    l_copy.wait()
    o_copy.wait()
    eye = ident[...].astype(F32)
    for g in range(GROUPS):
        at = pl.ds(g * QROWS, QROWS)
        level = jnp.sum(eye * l_recv[g : g + 1, :], axis=1, keepdims=True)
        mine = m_ref[0, at, :]
        top = jnp.maximum(mine, level)
        w_mine = jnp.exp2(mine - top)
        w_other = jnp.exp2(level - top)
        total = acc_ref[0, at, HD:] * w_mine + w_other
        o = acc_ref[0, at, :HD] * w_mine + o_recv[at, :].astype(F32) * w_other
        out_att[:, g * HD : (g + 1) * HD] = (o / total).astype(BF)


def on_device(*args):
    anywhere = pl.BlockSpec(memory_space=pl.ANY)
    vmem = pl.BlockSpec(memory_space=pltpu.VMEM)
    smem = pl.BlockSpec(memory_space=pltpu.SMEM)
    dma = pltpu.SemaphoreType.DMA
    return pl.pallas_call(
        kernel,
        out_shape=(
            jax.ShapeDtypeStruct((QROWS, GROUPS * HD), BF),
            jax.ShapeDtypeStruct((1, 64, 512), BF),
            jax.ShapeDtypeStruct((1, 4, 2048), BF),
        ),
        in_specs=[
            anywhere,
            anywhere,
            anywhere,
            anywhere,
            anywhere,
            smem,
            anywhere,
            smem,
            smem,
            anywhere,
            anywhere,
        ],
        out_specs=(vmem, vmem, vmem),
        scratch_shapes=[
            pltpu.VMEM((2, QROWS, GROUPS * HD), BF),
            pltpu.VMEM((ALL_ROWS, HD), BF),
            pltpu.VMEM((ALL_ROWS, HD), BF),
            pltpu.VMEM((ALL_ROWS + 2048, HD), BF),
            pltpu.VMEM((QROWS, HD), BF),
            pltpu.VMEM((2, GROUPS * QROWS, HD), F32),
            pltpu.VMEM((2, GROUPS * QROWS, 2 * HD), F32),
            pltpu.VMEM((GROUPS * QROWS, HD), BF),
            pltpu.VMEM((GROUPS * QROWS, HD), BF),
            pltpu.VMEM((GROUPS, HD), F32),
            pltpu.VMEM((GROUPS, HD), F32),
            pltpu.VMEM((2, 2, 64, HD), BF),
            pltpu.VMEM((4, 2048), BF),
            pltpu.VMEM((6, 512, 256), BF),
            pltpu.VMEM((6, 512, 256), BF),
            dma((32,)),
            dma((32,)),
            dma((32,)),
            dma((32,)),
            dma((5,)),
            dma((5,)),
            dma((10,)),
        ],
        compiler_params=pltpu.CompilerParams(
            collective_id=0, has_side_effects=True, vmem_limit_bytes=56 * 2**20
        ),
        cost_estimate=pl.CostEstimate(
            flops=12 * 10**9, bytes_accessed=8 * 10**6, transcendentals=22 * 10**6
        ),
    )(*args)


def solution(mesh):
    placed = (
        P(("seq", "rep"), "tp"),
        P(("seq", "rep"), "tp"),
        P(("seq", "rep"), "tp"),
        P(("seq", "rep"), "tp"),
        P(("seq", "rep"), "tp"),
        P(),
        P("tp", ("seq", "rep"), None),
        P(None, ("seq", "rep")),
        P(None, ("seq", "rep")),
        P("tp", ("seq", "rep"), None, None),
        P("tp", ("seq", "rep"), None, None),
    )
    return jax.shard_map(
        on_device,
        mesh=mesh,
        in_specs=placed,
        out_specs=(
            P(("seq", "rep"), "tp"),
            P("tp", ("seq", "rep"), None),
            P("tp", ("seq", "rep"), None),
        ),
        check_vma=False,
    )
```

```python
import jax
import jax.numpy as jnp
from jax import lax
from jax.experimental import pallas as pl
from jax.experimental.pallas import tpu as pltpu
from jax.sharding import PartitionSpec as P

HD = 128
GROUPS = 8
QROWS = 128
CROWS = 512
SHARD = CROWS + QROWS
PIECE = SHARD // 2
Z = 8
SCALE2 = 1.4426950408889634 / 128**0.5
MASKED = -1e31
M_START = -1e29
ALL_ROWS = 2 * Z * SHARD
TILE = 256
MESH = pl.DeviceIdType.MESH
BF = jnp.bfloat16
F32 = jnp.float32

SLOT_OF = ((0, 1, 3, 5, 7), (0, 2, 4, 6, 7))

STEPS = (
    (0, 0, 1280),
    (1, 0, 1280),
    (1, 1280, 1280),
    (0, 1280, 1280),
    (1, 2560, 2560),
    (0, 2560, 2560),
    (1, 5120, 2560),
    (1, 7680, 2560),
    (0, 5120, 2560),
    (0, 7680, 2560),
)
DUTIES = {
    0: ((0, 1, 0), (1, (0,))),
    1: ((2,),),
    2: ((0, 1, 1),),
    4: ((0, 2, 0), (0, 2, 1), (1, (1, 2))),
    5: ((0, 3, 0),),
    6: ((0, 3, 1), (1, (3, 4))),
    7: ((0, 4, 0), (1, (5, 6, 7))),
}
SEND_AFTER = 7


def base_of(slot, theirs):
    if slot == 0:
        return theirs * SHARD
    if slot == 7:
        return 7 * 2 * SHARD + theirs * SHARD
    return 2 * SHARD + ((slot - 1) // 2) * 4 * SHARD + ((slot - 1) % 2) * SHARD + theirs * 2 * SHARD


def pick(i, table):
    total = jnp.int32(0)
    for at, value in enumerate(table):
        if value:
            total = total + jnp.where(i == at, jnp.int32(value), jnp.int32(0))
    return total


def kernel(
    query,
    key_span,
    value_span,
    ctx_k,
    ctx_v,
    offset,
    dec_q,
    lengths,
    slots,
    cache_k,
    cache_v,
    out_att,
    out_hand,
    out_dec,
    qb,
    kv,
    mask,
    ident,
    m_ref,
    acc_ref,
    o_send,
    o_recv,
    l_send,
    l_recv,
    hbuf,
    dqb,
    ckb,
    cvb,
    ring_send,
    ring_recv,
    core_send,
    core_recv,
    misc_send,
    misc_recv,
    local_sem,
):
    z = lax.axis_index("seq")
    tp = lax.axis_index("tp")
    rep = lax.axis_index("rep")
    y = rep // 2
    c = rep % 2
    half = tp // 4
    nxt = {"seq": (z + 1) % Z}
    prv = {"seq": (z + Z - 1) % Z}
    core = {"rep": y * 2 + (1 - c)}
    other = {"rep": (1 - y) * 2 + c}
    mate = {"tp": (1 - half) * 4 + tp % 4}

    def held(slot, theirs, part):
        return kv.at[pl.ds(base_of(slot, theirs) + part * PIECE, PIECE), :]

    def ring(way, hop, turn):
        part = turn if way == 0 else 1 - turn
        at = (way * 4 + hop - 1) * 2 + turn
        return pltpu.make_async_remote_copy(
            src_ref=held(SLOT_OF[way][hop - 1], 0, part),
            dst_ref=held(SLOT_OF[way][hop], 0, part),
            send_sem=ring_send.at[at],
            recv_sem=ring_recv.at[at],
            device_id=nxt if way == 0 else prv,
            device_id_type=MESH,
        )

    def has_hop(hop, turn):
        return hop <= 3 or (hop == 4 and turn == 0)

    def across(slot, part):
        at = slot * 2 + part
        return pltpu.make_async_remote_copy(
            src_ref=held(slot, 0, part),
            dst_ref=held(slot, 1, part),
            send_sem=core_send.at[at],
            recv_sem=core_recv.at[at],
            device_id=core,
            device_id_type=MESH,
        )

    def pass_on(hop, turn):
        for way in (0, 1):
            ring(way, hop, turn).wait_recv()
            if has_hop(hop + 1, turn):
                ring(way, hop + 1, turn).start()
            across(SLOT_OF[way][hop], turn if way == 0 else 1 - turn).start()

    def misc(at, src, dst, device):
        return pltpu.make_async_remote_copy(
            src_ref=src,
            dst_ref=dst,
            send_sem=misc_send.at[at],
            recv_sem=misc_recv.at[at],
            device_id=device,
            device_id_type=MESH,
        )

    q_copy = misc(0, qb.at[0], qb.at[1], other)
    kept = pl.ds(pl.multiple_of(half * 64, 64), 64)
    given = pl.ds(pl.multiple_of(CROWS + (1 - half) * 64, 64), 64)
    h_copy = misc(1, kv.at[given, :], hbuf.at[half], mate)
    o_copy = misc(2, o_send, o_recv, other)
    l_copy = misc(3, l_send, l_recv, other)

    def run(todo):
        for what in todo:
            if what[0] == 0:
                pass_on(what[1], what[2])
            elif what[0] == 1:
                for slot in what[1]:
                    for part in (0, 1):
                        across(slot, part).wait_recv()
            else:
                q_copy.wait_recv()

    left, right = pl.ds(0, HD), pl.ds(HD, HD)
    local = [
        pltpu.make_async_copy(src, dst, local_sem.at[at])
        for at, (src, dst) in enumerate(
            (
                (ctx_k, kv.at[pl.ds(0, CROWS), left]),
                (ctx_v, kv.at[pl.ds(0, CROWS), right]),
                (key_span, kv.at[pl.ds(CROWS, QROWS), left]),
                (value_span, kv.at[pl.ds(CROWS, QROWS), right]),
                (query, qb.at[0]),
                (dec_q.at[0], dqb),
                (cache_k.at[0], ckb),
                (cache_v.at[0], cvb),
                (key_span.at[kept, :], hbuf.at[half, :, left]),
                (value_span.at[kept, :], hbuf.at[half, :, right]),
            )
        )
    ]
    barrier = pltpu.get_barrier_semaphore()
    for device in (nxt, prv, core, other, mate):
        pl.semaphore_signal(barrier, inc=1, device_id=device, device_id_type=MESH)
    for copy in local:
        copy.start()
    for copy in local[:5]:
        copy.wait()
    pl.semaphore_wait(barrier, 5)

    for turn in (0, 1):
        for way in (0, 1):
            ring(way, 1, turn).start()
    for part in (0, 1):
        across(0, part).start()
    q_copy.start()
    h_copy.start()

    row = lax.broadcasted_iota(jnp.int32, (QROWS, HD), 0)
    col = lax.broadcasted_iota(jnp.int32, (QROWS, HD), 1)
    ident[...] = jnp.where(row == col, 1.0, 0.0).astype(BF)
    limit = offset[0]
    long_row = lax.broadcasted_iota(jnp.int32, (CROWS, HD), 0)

    def fill(slot, carry):
        odd = slot % 2
        z_slot = (z + 2 * Z - odd * ((slot + 1) // 2) + (1 - odd) * (slot // 2)) % Z
        for theirs in (0, 1):
            block = z_slot * 4 + y * 2 + (c if theirs == 0 else 1 - c)
            base = jnp.where(
                (slot > 0) & (slot < 7),
                2 * SHARD
                + ((slot + 1) // 2 - 1) * 4 * SHARD
                + (1 - odd) * SHARD
                + theirs * 2 * SHARD,
                slot * 2 * SHARD + theirs * SHARD,
            )
            base = pl.multiple_of(base, QROWS)
            long = jnp.where(long_row + block * CROWS >= limit, MASKED, 0.0).astype(BF)
            for b in (0, 1):
                y_b = y if b == 0 else 1 - y
                ahead = (block - (z * 4 + y_b * 2 + c)) * QROWS
                mask[b, pl.ds(base, CROWS), :] = long
                mask[b, pl.ds(base + CROWS, QROWS), :] = jnp.where(
                    row + ahead > col, MASKED, 0.0
                ).astype(BF)
        return carry

    lax.fori_loop(0, 8, fill, 0)
    m_ref[...] = jnp.full_like(m_ref, M_START)
    acc_ref[...] = jnp.zeros_like(acc_ref)

    for copy in local[5:]:
        copy.wait()
    dq = dqb[...].astype(F32)
    picked = [slots[half, b] for b in range(4)]
    live = [lengths[half, b] for b in range(4)]
    place = lax.broadcasted_iota(jnp.int32, (64, 512), 1)
    request = lax.broadcasted_iota(jnp.int32, (64, 512), 0) % 8
    ok = jnp.concatenate(
        [(request == b) & (place < live[b]) for b in range(4)], axis=1
    )
    blank = jnp.zeros((4, HD), F32)
    for head in (0, 1):
        lanes = slice(head * HD, (head + 1) * HD)
        q = jnp.concatenate(
            [
                part
                for g in range(GROUPS)
                for part in (dq[:, (head * 8 + g) * HD : (head * 8 + g + 1) * HD], blank)
            ],
            axis=0,
        ).astype(BF)
        k = jnp.concatenate([ckb[picked[b]][:, lanes] for b in range(4)], axis=0)
        v = jnp.concatenate([cvb[picked[b]][:, lanes] for b in range(4)], axis=0)
        s = lax.dot_general(q, k, (((1,), (1,)), ((), ())), preferred_element_type=F32)
        s = jnp.where(ok, s * SCALE2, MASKED)
        top = jnp.max(s, axis=1, keepdims=True)
        w = jnp.where(ok, jnp.exp2(s - top), 0.0)
        total = jnp.sum(w, axis=1, keepdims=True)
        o = lax.dot_general(
            w.astype(BF), v, (((1,), (0,)), ((), ())), preferred_element_type=F32
        )
        o = o / total
        for g in range(GROUPS):
            out_dec[0, :, (head * 8 + g) * HD : (head * 8 + g + 1) * HD] = o[
                g * 8 : g * 8 + 4, :
            ].astype(BF)

    def scores_block(b, key_off, width):
        keys = pl.ds(pl.multiple_of(key_off, 256), width)
        k = jnp.concatenate([kv[keys, :HD], mask[b, keys, :]], axis=1)
        v = jnp.concatenate([kv[keys, HD:], jnp.ones((width, HD), BF)], axis=1)
        eye = jnp.concatenate([ident[...]] * 2, axis=0)
        all_s = []
        for t in range(4):
            q = jnp.concatenate(
                [qb[b, :, (2 * t + u) * HD : (2 * t + u + 1) * HD] for u in (0, 1)], axis=0
            )
            q = jnp.concatenate([q, eye], axis=1)
            all_s.append(
                lax.dot_general(q, k, (((1,), (1,)), ((), ())), preferred_element_type=F32)
            )
        for t in range(4):
            s = all_s[t]
            at = pl.ds(t * TILE, TILE)
            before = m_ref[b, at, :]
            now = jnp.maximum(before, jnp.max(s, axis=1, keepdims=True) * SCALE2)
            factor = jnp.exp2(before - now)
            p = jnp.exp2(s * SCALE2 - now[:, :1])
            m_ref[b, at, :] = now
            pv = lax.dot_general(
                p.astype(BF), v, (((1,), (0,)), ((), ())), preferred_element_type=F32
            )
            acc_ref[b, at, :] = acc_ref[b, at, :] * jnp.concatenate([factor, factor], axis=1) + pv

    def one_step(i, carry):
        for step, todo in DUTIES.items():
            pl.when(i == step)(lambda todo=todo: run(todo))
        b = pick(i, [s[0] for s in STEPS])
        off = pick(i, [s[1] for s in STEPS])
        short = pick(i, [int(s[2] == 1280) for s in STEPS])
        pl.when(short == 1)(lambda: scores_block(b, off, 1280))
        pl.when(short == 0)(lambda: scores_block(b, off, 2560))

        @pl.when(i == SEND_AFTER)
        def _():
            eye = ident[...].astype(F32)
            for g in range(GROUPS):
                at = pl.ds(g * QROWS, QROWS)
                total = acc_ref[1, at, HD:]
                o_send[at, :] = (acc_ref[1, at, :HD] / total).astype(BF)
                level = m_ref[1, at, :] + jnp.log(total) * 1.4426950408889634
                l_send[g : g + 1, :] = jnp.sum(level * eye, axis=0, keepdims=True)
            l_copy.start()
            o_copy.start()

        return carry

    lax.fori_loop(0, len(STEPS), one_step, 0)

    h_copy.wait()
    for u in (0, 1):
        out_hand[0, :, u * 2 * HD : (u + 1) * 2 * HD] = hbuf[u]
    for hop in (1, 2, 3, 4):
        for turn in (0, 1):
            for way in (0, 1):
                if has_hop(hop, turn):
                    ring(way, hop, turn).wait_send()
    for slot in range(8):
        for part in (0, 1):
            across(slot, part).wait_send()
    q_copy.wait_send()
    l_copy.wait()
    o_copy.wait()
    eye = ident[...].astype(F32)
    for g in range(GROUPS):
        at = pl.ds(g * QROWS, QROWS)
        level = jnp.sum(eye * l_recv[g : g + 1, :], axis=1, keepdims=True)
        mine = m_ref[0, at, :]
        top = jnp.maximum(mine, level)
        w_mine = jnp.exp2(mine - top)
        w_other = jnp.exp2(level - top)
        total = acc_ref[0, at, HD:] * w_mine + w_other
        o = acc_ref[0, at, :HD] * w_mine + o_recv[at, :].astype(F32) * w_other
        out_att[:, g * HD : (g + 1) * HD] = (o / total).astype(BF)


def deliver(a, b, c, out_a, out_b, out_c):
    out_a[...] = a[...]
    out_b[...] = b[...]
    out_c[...] = c[...]


def on_device(*args):
    anywhere = pl.BlockSpec(memory_space=pl.ANY)
    vmem = pl.BlockSpec(memory_space=pltpu.VMEM)
    smem = pl.BlockSpec(memory_space=pltpu.SMEM)
    dma = pltpu.SemaphoreType.DMA
    shapes = (
        jax.ShapeDtypeStruct((QROWS, GROUPS * HD), BF),
        jax.ShapeDtypeStruct((1, 64, 512), BF),
        jax.ShapeDtypeStruct((1, 4, 2048), BF),
    )
    results = pl.pallas_call(
        kernel,
        out_shape=shapes,
        in_specs=[
            anywhere,
            anywhere,
            anywhere,
            anywhere,
            anywhere,
            smem,
            anywhere,
            smem,
            smem,
            anywhere,
            anywhere,
        ],
        out_specs=(vmem, vmem, vmem),
        scratch_shapes=[
            pltpu.VMEM((2, QROWS, GROUPS * HD), BF),
            pltpu.VMEM((ALL_ROWS, 2 * HD), BF),
            pltpu.VMEM((2, ALL_ROWS, HD), BF),
            pltpu.VMEM((QROWS, HD), BF),
            pltpu.VMEM((2, GROUPS * QROWS, HD), F32),
            pltpu.VMEM((2, GROUPS * QROWS, 2 * HD), F32),
            pltpu.VMEM((GROUPS * QROWS, HD), BF),
            pltpu.VMEM((GROUPS * QROWS, HD), BF),
            pltpu.VMEM((GROUPS, HD), F32),
            pltpu.VMEM((GROUPS, HD), F32),
            pltpu.VMEM((2, 64, 2 * HD), BF),
            pltpu.VMEM((4, 2048), BF),
            pltpu.VMEM((6, 512, 256), BF),
            pltpu.VMEM((6, 512, 256), BF),
            dma((16,)),
            dma((16,)),
            dma((16,)),
            dma((16,)),
            dma((4,)),
            dma((4,)),
            dma((10,)),
        ],
        compiler_params=pltpu.CompilerParams(
            collective_id=0, has_side_effects=True, vmem_limit_bytes=56 * 2**20
        ),
        cost_estimate=pl.CostEstimate(
            flops=12 * 10**9, bytes_accessed=8 * 10**6, transcendentals=22 * 10**6
        ),
    )(*args)
    return pl.pallas_call(
        deliver,
        out_shape=shapes,
        in_specs=[vmem] * 3,
        out_specs=(vmem,) * 3,
    )(*results)


def solution(mesh):
    placed = (
        P(("seq", "rep"), "tp"),
        P(("seq", "rep"), "tp"),
        P(("seq", "rep"), "tp"),
        P(("seq", "rep"), "tp"),
        P(("seq", "rep"), "tp"),
        P(),
        P("tp", ("seq", "rep"), None),
        P(None, ("seq", "rep")),
        P(None, ("seq", "rep")),
        P("tp", ("seq", "rep"), None, None),
        P("tp", ("seq", "rep"), None, None),
    )
    return jax.shard_map(
        on_device,
        mesh=mesh,
        in_specs=placed,
        out_specs=(
            P(("seq", "rep"), "tp"),
            P("tp", ("seq", "rep"), None),
            P("tp", ("seq", "rep"), None),
        ),
        check_vma=False,
    )
```

```python
import jax
import jax.numpy as jnp
from jax import lax
from jax.experimental import pallas as pl
from jax.experimental.pallas import tpu as pltpu
from jax.sharding import PartitionSpec as P

HD = 128
GROUPS = 8
QROWS = 128
CROWS = 512
PIECE = CROWS // 2
Z = 8
SCALE2 = 1.4426950408889634 / 128**0.5
MASKED = -1e31
M_START = -1e29
ALL_ROWS = 2 * Z * (CROWS + QROWS)
TILE = 256
MESH = pl.DeviceIdType.MESH
BF = jnp.bfloat16
F32 = jnp.float32

SLOT_OF = ((0, 1, 3, 5, 7), (0, 2, 4, 6, 7))

STEPS = (
    (0, 0, 1280, -1),
    (1, 0, 1280, -1),
    (1, 1280, 1280, 0),
    (0, 1280, 1280, 0),
    (1, 2560, 2560, 0),
    (0, 2560, 2560, 0),
    (1, 5120, 2560, 1),
    (1, 7680, 2560, 2),
    (0, 5120, 2560, 1),
    (0, 7680, 2560, 2),
)
DUTIES = {
    0: ((0, 1, 0), (1, (0,))),
    1: ((3, 1), (2,)),
    2: ((0, 1, 1),),
    4: ((0, 2, 0), (3, 2), (0, 2, 1), (1, (1, 2))),
    5: ((0, 3, 0), (3, 3)),
    6: ((0, 3, 1), (1, (3, 4))),
    7: ((0, 4, 0), (3, 4), (1, (5, 6, 7))),
}
SEND_AFTER = 7


def base_of(slot, theirs):
    if slot == 0:
        return theirs * 512
    if slot == 7:
        return 8704 + theirs * 512
    pair, second = (slot - 1) // 2, (slot - 1) % 2
    if theirs:
        return 2560 * (pair + 1) + second * 512
    return (1280 if pair == 0 else 2560 * pair + 1024) + second * 512


def span_base_of(slot, theirs):
    if slot == 0:
        return 1024 + theirs * 128
    if slot == 7:
        return 9984 + theirs * 128
    pair, second = (slot - 1) // 2, (slot - 1) % 2
    if theirs:
        return 2560 * (pair + 1) + 2048 + second * 128
    return 2304 + 2560 * pair + second * 128


def pick(i, table):
    total = jnp.int32(0)
    for at, value in enumerate(table):
        if value:
            total = total + jnp.where(i == at, jnp.int32(value), jnp.int32(0))
    return total


def kernel(
    query,
    key_span,
    value_span,
    ctx_k,
    ctx_v,
    offset,
    dec_q,
    lengths,
    slots,
    cache_k,
    cache_v,
    out_att,
    out_hand,
    out_dec,
    qb,
    kv,
    mask,
    ident,
    m_ref,
    acc_ref,
    o_send,
    o_recv,
    l_send,
    l_recv,
    hbuf,
    dqb,
    ckb,
    cvb,
    ring_send,
    ring_recv,
    core_send,
    core_recv,
    span_send,
    span_recv,
    pair_send,
    pair_recv,
    misc_send,
    misc_recv,
    local_sem,
):
    z = lax.axis_index("seq")
    tp = lax.axis_index("tp")
    rep = lax.axis_index("rep")
    y = rep // 2
    c = rep % 2
    half = tp // 4
    nxt = {"seq": (z + 1) % Z}
    prv = {"seq": (z + Z - 1) % Z}
    core = {"rep": y * 2 + (1 - c)}
    other = {"rep": (1 - y) * 2 + c}
    mate = {"tp": (1 - half) * 4 + tp % 4}

    def held(slot, theirs, part):
        return kv.at[pl.ds(base_of(slot, theirs) + part * PIECE, PIECE), :]

    def ring(way, hop, turn):
        part = turn if way == 0 else 1 - turn
        at = (way * 4 + hop - 1) * 2 + turn
        return pltpu.make_async_remote_copy(
            src_ref=held(SLOT_OF[way][hop - 1], 0, part),
            dst_ref=held(SLOT_OF[way][hop], 0, part),
            send_sem=ring_send.at[at],
            recv_sem=ring_recv.at[at],
            device_id=nxt if way == 0 else prv,
            device_id_type=MESH,
        )

    def has_hop(hop, turn):
        return hop <= 3 or (hop == 4 and turn == 0)

    def across(slot, part):
        at = slot * 2 + part
        return pltpu.make_async_remote_copy(
            src_ref=held(slot, 0, part),
            dst_ref=held(slot, 1, part),
            send_sem=core_send.at[at],
            recv_sem=core_recv.at[at],
            device_id=core,
            device_id_type=MESH,
        )

    def pass_on(hop, turn):
        for way in (0, 1):
            ring(way, hop, turn).wait_recv()
            if has_hop(hop + 1, turn):
                ring(way, hop + 1, turn).start()
            across(SLOT_OF[way][hop], turn if way == 0 else 1 - turn).start()

    def span_rows(slot, theirs):
        return kv.at[pl.ds(span_base_of(slot, theirs), QROWS), :]

    def span_ring(way, hop):
        return pltpu.make_async_remote_copy(
            src_ref=span_rows(SLOT_OF[way][hop - 1], 0),
            dst_ref=span_rows(SLOT_OF[way][hop], 0),
            send_sem=span_send.at[way * 4 + hop - 1],
            recv_sem=span_recv.at[way * 4 + hop - 1],
            device_id=nxt if way == 0 else prv,
            device_id_type=MESH,
        )

    def span_comes(way, hop):
        return z >= hop if way == 0 else (z + hop) % Z <= 2

    def span_goes(way, hop):
        return (z + 1) % Z >= hop if way == 0 else (z + hop - 1) % Z <= 2

    def span_hops():
        return [(0, 1), (1, 1), (0, 2), (1, 2), (0, 3), (1, 3), (0, 4)]

    def span_across(way, hop):
        slot = SLOT_OF[way][hop]
        return pltpu.make_async_remote_copy(
            src_ref=span_rows(slot, 0),
            dst_ref=span_rows(slot, 1),
            send_sem=pair_send.at[slot],
            recv_sem=pair_recv.at[slot],
            device_id=core,
            device_id_type=MESH,
        )

    def pass_span(hop):
        for way in (0, 1):
            if (way, hop) in span_hops():

                @pl.when(span_comes(way, hop))
                def _(way=way):
                    span_ring(way, hop).wait_recv()
                    span_across(way, hop).start()

                if (way, hop + 1) in span_hops():

                    @pl.when(span_goes(way, hop + 1))
                    def _(way=way):
                        span_ring(way, hop + 1).start()

    def misc(at, src, dst, device):
        return pltpu.make_async_remote_copy(
            src_ref=src,
            dst_ref=dst,
            send_sem=misc_send.at[at],
            recv_sem=misc_recv.at[at],
            device_id=device,
            device_id_type=MESH,
        )

    q_copy = misc(0, qb.at[0], qb.at[1], other)
    kept = pl.ds(pl.multiple_of(half * 64, 64), 64)
    mine = pl.ds(span_base_of(0, 0), QROWS)
    given = pl.ds(pl.multiple_of(span_base_of(0, 0) + (1 - half) * 64, 64), 64)
    h_copy = misc(1, kv.at[given, :], hbuf.at[half], mate)
    o_copy = misc(2, o_send, o_recv, other)
    l_copy = misc(3, l_send, l_recv, other)

    def run(todo):
        for what in todo:
            if what[0] == 0:
                pass_on(what[1], what[2])
            elif what[0] == 1:
                for slot in what[1]:
                    for part in (0, 1):
                        across(slot, part).wait_recv()
                    if slot == 0:
                        span_across(0, 0).wait_recv()
                    for way, hop in span_hops():
                        if SLOT_OF[way][hop] == slot:

                            @pl.when(span_comes(way, hop))
                            def _(way=way, hop=hop):
                                span_across(way, hop).wait_recv()

            elif what[0] == 2:
                q_copy.wait_recv()
            else:
                pass_span(what[1])

    left, right = pl.ds(0, HD), pl.ds(HD, HD)
    local = [
        pltpu.make_async_copy(src, dst, local_sem.at[at])
        for at, (src, dst) in enumerate(
            (
                (ctx_k, kv.at[pl.ds(0, CROWS), left]),
                (ctx_v, kv.at[pl.ds(0, CROWS), right]),
                (key_span, kv.at[mine, left]),
                (value_span, kv.at[mine, right]),
                (query, qb.at[0]),
                (dec_q.at[0], dqb),
                (cache_k.at[0], ckb),
                (cache_v.at[0], cvb),
                (key_span.at[kept, :], hbuf.at[half, :, left]),
                (value_span.at[kept, :], hbuf.at[half, :, right]),
            )
        )
    ]
    barrier = pltpu.get_barrier_semaphore()
    for device in (nxt, prv, core, other, mate):
        pl.semaphore_signal(barrier, inc=1, device_id=device, device_id_type=MESH)
    for copy in local:
        copy.start()
    for copy in local[:5]:
        copy.wait()
    pl.semaphore_wait(barrier, 5)

    for way in (0, 1):
        ring(way, 1, 0).start()
    for way in (0, 1):
        pl.when(span_goes(way, 1))(lambda way=way: span_ring(way, 1).start())
    for way in (0, 1):
        ring(way, 1, 1).start()
    for part in (0, 1):
        across(0, part).start()
    span_across(0, 0).start()
    q_copy.start()
    h_copy.start()

    row = lax.broadcasted_iota(jnp.int32, (QROWS, HD), 0)
    col = lax.broadcasted_iota(jnp.int32, (QROWS, HD), 1)
    ident[...] = jnp.where(row == col, 1.0, 0.0).astype(BF)
    limit = offset[0]
    long_row = lax.broadcasted_iota(jnp.int32, (CROWS, HD), 0)

    for slot in range(8):
        way, hop = (0, (slot + 1) // 2) if slot % 2 or slot == 0 else (1, slot // 2)
        z_slot = (z + Z - hop) % Z if way == 0 else (z + hop) % Z
        for theirs in (0, 1):
            block = z_slot * 4 + y * 2 + (c if theirs == 0 else 1 - c)
            far = pl.ds(base_of(slot, theirs), CROWS)
            near = pl.ds(span_base_of(slot, theirs), QROWS)
            long = jnp.where(long_row + block * CROWS >= limit, MASKED, 0.0).astype(BF)
            for b in (0, 1):
                y_b = y if b == 0 else 1 - y
                ahead = (block - (z * 4 + y_b * 2 + c)) * QROWS
                mask[b, far, :] = long
                mask[b, near, :] = jnp.where(row + ahead > col, MASKED, 0.0).astype(BF)

            if slot:

                @pl.when(jnp.logical_not(span_comes(way, hop)))
                def _(near=near):
                    kv[near, :] = jnp.zeros((QROWS, 2 * HD), BF)

    m_ref[...] = jnp.full_like(m_ref, M_START)
    acc_ref[...] = jnp.zeros_like(acc_ref)

    for copy in local[5:]:
        copy.wait()
    dq = dqb[...].astype(F32)
    picked = [slots[half, b] for b in range(4)]
    live = [lengths[half, b] for b in range(4)]
    place = lax.broadcasted_iota(jnp.int32, (64, 512), 1)
    request = lax.broadcasted_iota(jnp.int32, (64, 512), 0) % 8
    ok = jnp.concatenate(
        [(request == b) & (place < live[b]) for b in range(4)], axis=1
    )
    blank = jnp.zeros((4, HD), F32)
    for head in (0, 1):
        lanes = slice(head * HD, (head + 1) * HD)
        q = jnp.concatenate(
            [
                part
                for g in range(GROUPS)
                for part in (dq[:, (head * 8 + g) * HD : (head * 8 + g + 1) * HD], blank)
            ],
            axis=0,
        ).astype(BF)
        k = jnp.concatenate([ckb[picked[b]][:, lanes] for b in range(4)], axis=0)
        v = jnp.concatenate([cvb[picked[b]][:, lanes] for b in range(4)], axis=0)
        s = lax.dot_general(q, k, (((1,), (1,)), ((), ())), preferred_element_type=F32)
        s = jnp.where(ok, s * SCALE2, MASKED)
        top = jnp.max(s, axis=1, keepdims=True)
        w = jnp.where(ok, jnp.exp2(s - top), 0.0)
        total = jnp.sum(w, axis=1, keepdims=True)
        o = lax.dot_general(
            w.astype(BF), v, (((1,), (0,)), ((), ())), preferred_element_type=F32
        )
        o = o / total
        for g in range(GROUPS):
            out_dec[0, :, (head * 8 + g) * HD : (head * 8 + g + 1) * HD] = o[
                g * 8 : g * 8 + 4, :
            ].astype(BF)

    def scores_block(b, key_off, width):
        keys = pl.ds(pl.multiple_of(key_off, 256), width)
        k = jnp.concatenate([kv[keys, :HD], mask[b, keys, :]], axis=1)
        v = jnp.concatenate([kv[keys, HD:], jnp.ones((width, HD), BF)], axis=1)
        eye = jnp.concatenate([ident[...]] * 2, axis=0)
        all_s = []
        for t in range(4):
            q = jnp.concatenate(
                [qb[b, :, (2 * t + u) * HD : (2 * t + u + 1) * HD] for u in (0, 1)], axis=0
            )
            q = jnp.concatenate([q, eye], axis=1)
            all_s.append(
                lax.dot_general(q, k, (((1,), (1,)), ((), ())), preferred_element_type=F32)
            )
        for t in range(4):
            s = all_s[t]
            at = pl.ds(t * TILE, TILE)
            before = m_ref[b, at, :]
            now = jnp.maximum(before, jnp.max(s, axis=1, keepdims=True) * SCALE2)
            factor = jnp.exp2(before - now)
            p = jnp.exp2(s * SCALE2 - now[:, :1])
            m_ref[b, at, :] = now
            pv = lax.dot_general(
                p.astype(BF), v, (((1,), (0,)), ((), ())), preferred_element_type=F32
            )
            acc_ref[b, at, :] = acc_ref[b, at, :] * jnp.concatenate([factor, factor], axis=1) + pv

    def one_step(i, carry):
        for step, todo in DUTIES.items():
            pl.when(i == step)(lambda todo=todo: run(todo))
        b = pick(i, [s[0] for s in STEPS])
        off = pick(i, [s[1] for s in STEPS])
        width = pick(i, [s[2] for s in STEPS])
        spare = pick(i, [s[3] + 1 for s in STEPS])
        width = jnp.where(z < spare, (width // 5) * 4, width)
        for size in (1024, 1280, 2048, 2560):
            pl.when(width == size)(lambda size=size: scores_block(b, off, size))

        @pl.when(i == SEND_AFTER)
        def _():
            eye = ident[...].astype(F32)
            for g in range(GROUPS):
                at = pl.ds(g * QROWS, QROWS)
                total = acc_ref[1, at, HD:]
                o_send[at, :] = (acc_ref[1, at, :HD] / total).astype(BF)
                level = m_ref[1, at, :] + jnp.log(total) * 1.4426950408889634
                l_send[g : g + 1, :] = jnp.sum(level * eye, axis=0, keepdims=True)
            l_copy.start()
            o_copy.start()

        return carry

    lax.fori_loop(0, len(STEPS), one_step, 0)

    h_copy.wait()
    for u in (0, 1):
        out_hand[0, :, u * 2 * HD : (u + 1) * 2 * HD] = hbuf[u]
    for hop in (1, 2, 3, 4):
        for turn in (0, 1):
            for way in (0, 1):
                if has_hop(hop, turn):
                    ring(way, hop, turn).wait_send()
    for slot in range(8):
        for part in (0, 1):
            across(slot, part).wait_send()
    span_across(0, 0).wait_send()
    for way, hop in span_hops():
        pl.when(span_goes(way, hop))(lambda way=way, hop=hop: span_ring(way, hop).wait_send())
        pl.when(span_comes(way, hop))(lambda way=way, hop=hop: span_across(way, hop).wait_send())
    q_copy.wait_send()
    l_copy.wait()
    o_copy.wait()
    eye = ident[...].astype(F32)
    for g in range(GROUPS):
        at = pl.ds(g * QROWS, QROWS)
        level = jnp.sum(eye * l_recv[g : g + 1, :], axis=1, keepdims=True)
        mine = m_ref[0, at, :]
        top = jnp.maximum(mine, level)
        w_mine = jnp.exp2(mine - top)
        w_other = jnp.exp2(level - top)
        total = acc_ref[0, at, HD:] * w_mine + w_other
        o = acc_ref[0, at, :HD] * w_mine + o_recv[at, :].astype(F32) * w_other
        out_att[:, g * HD : (g + 1) * HD] = (o / total).astype(BF)


def deliver(a, b, c, out_a, out_b, out_c):
    out_a[...] = a[...]
    out_b[...] = b[...]
    out_c[...] = c[...]


def on_device(*args):
    anywhere = pl.BlockSpec(memory_space=pl.ANY)
    vmem = pl.BlockSpec(memory_space=pltpu.VMEM)
    smem = pl.BlockSpec(memory_space=pltpu.SMEM)
    dma = pltpu.SemaphoreType.DMA
    shapes = (
        jax.ShapeDtypeStruct((QROWS, GROUPS * HD), BF),
        jax.ShapeDtypeStruct((1, 64, 512), BF),
        jax.ShapeDtypeStruct((1, 4, 2048), BF),
    )
    results = pl.pallas_call(
        kernel,
        out_shape=shapes,
        in_specs=[
            anywhere,
            anywhere,
            anywhere,
            anywhere,
            anywhere,
            smem,
            anywhere,
            smem,
            smem,
            anywhere,
            anywhere,
        ],
        out_specs=(vmem, vmem, vmem),
        scratch_shapes=[
            pltpu.VMEM((2, QROWS, GROUPS * HD), BF),
            pltpu.VMEM((ALL_ROWS, 2 * HD), BF),
            pltpu.VMEM((2, ALL_ROWS, HD), BF),
            pltpu.VMEM((QROWS, HD), BF),
            pltpu.VMEM((2, GROUPS * QROWS, HD), F32),
            pltpu.VMEM((2, GROUPS * QROWS, 2 * HD), F32),
            pltpu.VMEM((GROUPS * QROWS, HD), BF),
            pltpu.VMEM((GROUPS * QROWS, HD), BF),
            pltpu.VMEM((GROUPS, HD), F32),
            pltpu.VMEM((GROUPS, HD), F32),
            pltpu.VMEM((2, 64, 2 * HD), BF),
            pltpu.VMEM((4, 2048), BF),
            pltpu.VMEM((6, 512, 256), BF),
            pltpu.VMEM((6, 512, 256), BF),
            dma((16,)),
            dma((16,)),
            dma((16,)),
            dma((16,)),
            dma((8,)),
            dma((8,)),
            dma((8,)),
            dma((8,)),
            dma((4,)),
            dma((4,)),
            dma((10,)),
        ],
        compiler_params=pltpu.CompilerParams(
            collective_id=0, has_side_effects=True, vmem_limit_bytes=56 * 2**20
        ),
        cost_estimate=pl.CostEstimate(
            flops=12 * 10**9, bytes_accessed=8 * 10**6, transcendentals=22 * 10**6
        ),
    )(*args)
    return pl.pallas_call(
        deliver,
        out_shape=shapes,
        in_specs=[vmem] * 3,
        out_specs=(vmem,) * 3,
    )(*results)


def solution(mesh):
    placed = (
        P(("seq", "rep"), "tp"),
        P(("seq", "rep"), "tp"),
        P(("seq", "rep"), "tp"),
        P(("seq", "rep"), "tp"),
        P(("seq", "rep"), "tp"),
        P(),
        P("tp", ("seq", "rep"), None),
        P(None, ("seq", "rep")),
        P(None, ("seq", "rep")),
        P("tp", ("seq", "rep"), None, None),
        P("tp", ("seq", "rep"), None, None),
    )
    return jax.shard_map(
        on_device,
        mesh=mesh,
        in_specs=placed,
        out_specs=(
            P(("seq", "rep"), "tp"),
            P("tp", ("seq", "rep"), None),
            P("tp", ("seq", "rep"), None),
        ),
        check_vma=False,
    )
```

```python
import jax
import jax.numpy as jnp
from jax import lax
from jax.experimental import pallas as pl
from jax.experimental.pallas import tpu as pltpu
from jax.sharding import PartitionSpec as P

HD = 128
GROUPS = 8
QROWS = 128
CROWS = 512
PIECE = CROWS // 2
Z = 8
SCALE2 = 1.4426950408889634 / 128**0.5
MASKED = -1e31
M_START = -1e29
ALL_ROWS = 2 * Z * (CROWS + QROWS)
TILE = 256
MESH = pl.DeviceIdType.MESH
BF = jnp.bfloat16
F32 = jnp.float32

SLOT_OF = ((0, 1, 3, 5, 7), (0, 2, 4, 6, 7))

STEPS = (
    (0, 0, 1280, -1, 0),
    (1, 0, 1280, -1, 0),
    (1, 1280, 1280, 0, 0),
    (0, 1280, 1280, 0, 0),
    (1, 2560, 1280, 0, 256),
    (1, 3840, 1280, 1, 0),
    (0, 2560, 2560, 0, 256),
    (1, 5120, 1280, 1, 256),
    (1, 6400, 1280, 2, 0),
    (1, 7680, 1280, 2, 256),
    (1, 8960, 1280, 3, 0),
    (0, 5120, 2560, 1, 256),
    (0, 7680, 2560, 2, 256),
)
DUTIES = {
    0: ((1, (0,)),),
    1: ((0, 1, 0), (3, 1), (2,)),
    2: ((0, 1, 1),),
    4: ((0, 2, 0), (3, 2), (1, (1, 2))),
    5: ((0, 2, 1),),
    7: ((0, 3, 0), (3, 3), (1, (3, 4))),
    8: ((0, 3, 1),),
    9: ((0, 4, 0), (1, (5, 6))),
    10: ((3, 4), (1, (7,))),
}
SEND_AFTER = 10


def base_of(slot, theirs):
    if slot == 0:
        return theirs * 512
    if slot == 7:
        return 8960 + theirs * 512
    pair, second = (slot - 1) // 2, (slot - 1) % 2
    if theirs:
        return 2560 * (pair + 1) + 256 + second * 512
    return 1280 + 2560 * pair + second * 512


def span_base_of(slot, theirs):
    if slot == 0:
        return 1024 + theirs * 128
    if slot == 7:
        return 9984 + theirs * 128
    pair, second = (slot - 1) // 2, (slot - 1) % 2
    if theirs:
        return 2560 * (pair + 1) + second * 128
    return 2304 + 2560 * pair + second * 128


def pick(i, table):
    total = jnp.int32(0)
    for at, value in enumerate(table):
        if value:
            total = total + jnp.where(i == at, jnp.int32(value), jnp.int32(0))
    return total


def kernel(
    query,
    key_span,
    value_span,
    ctx_k,
    ctx_v,
    offset,
    dec_q,
    lengths,
    slots,
    cache_k,
    cache_v,
    out_att,
    out_hand,
    out_dec,
    qb,
    kv,
    mask,
    ident,
    m_ref,
    acc_ref,
    o_send,
    o_recv,
    l_send,
    l_recv,
    hbuf,
    dqb,
    ckb,
    cvb,
    ring_send,
    ring_recv,
    core_send,
    core_recv,
    span_send,
    span_recv,
    pair_send,
    pair_recv,
    misc_send,
    misc_recv,
    local_sem,
):
    z = lax.axis_index("seq")
    tp = lax.axis_index("tp")
    rep = lax.axis_index("rep")
    y = rep // 2
    c = rep % 2
    half = tp // 4
    nxt = {"seq": (z + 1) % Z}
    prv = {"seq": (z + Z - 1) % Z}
    core = {"rep": y * 2 + (1 - c)}
    other = {"rep": (1 - y) * 2 + c}
    mate = {"tp": (1 - half) * 4 + tp % 4}

    def held(slot, theirs, part):
        return kv.at[pl.ds(base_of(slot, theirs) + part * PIECE, PIECE), :]

    def ring(way, hop, turn):
        part = turn if way == 0 else 1 - turn
        at = (way * 4 + hop - 1) * 2 + turn
        return pltpu.make_async_remote_copy(
            src_ref=held(SLOT_OF[way][hop - 1], 0, part),
            dst_ref=held(SLOT_OF[way][hop], 0, part),
            send_sem=ring_send.at[at],
            recv_sem=ring_recv.at[at],
            device_id=nxt if way == 0 else prv,
            device_id_type=MESH,
        )

    def has_hop(hop, turn):
        return hop <= 3 or (hop == 4 and turn == 0)

    def across(slot, part):
        at = slot * 2 + part
        return pltpu.make_async_remote_copy(
            src_ref=held(slot, 0, part),
            dst_ref=held(slot, 1, part),
            send_sem=core_send.at[at],
            recv_sem=core_recv.at[at],
            device_id=core,
            device_id_type=MESH,
        )

    def pass_on(hop, turn):
        for way in (0, 1):
            ring(way, hop, turn).wait_recv()
            if has_hop(hop + 1, turn):
                ring(way, hop + 1, turn).start()
            across(SLOT_OF[way][hop], turn if way == 0 else 1 - turn).start()

    def span_rows(slot, theirs):
        return kv.at[pl.ds(span_base_of(slot, theirs), QROWS), :]

    def span_ring(way, hop):
        return pltpu.make_async_remote_copy(
            src_ref=span_rows(SLOT_OF[way][hop - 1], 0),
            dst_ref=span_rows(SLOT_OF[way][hop], 0),
            send_sem=span_send.at[way * 4 + hop - 1],
            recv_sem=span_recv.at[way * 4 + hop - 1],
            device_id=nxt if way == 0 else prv,
            device_id_type=MESH,
        )

    def span_comes(way, hop):
        return z >= hop if way == 0 else (z + hop) % Z <= 2

    def span_goes(way, hop):
        return (z + 1) % Z >= hop if way == 0 else (z + hop - 1) % Z <= 2

    def span_hops():
        return [(0, 1), (1, 1), (0, 2), (1, 2), (0, 3), (1, 3), (0, 4)]

    def span_across(way, hop):
        slot = SLOT_OF[way][hop]
        return pltpu.make_async_remote_copy(
            src_ref=span_rows(slot, 0),
            dst_ref=span_rows(slot, 1),
            send_sem=pair_send.at[slot],
            recv_sem=pair_recv.at[slot],
            device_id=core,
            device_id_type=MESH,
        )

    def pass_span(hop):
        for way in (0, 1):
            if (way, hop) in span_hops():

                @pl.when(span_comes(way, hop))
                def _(way=way):
                    span_ring(way, hop).wait_recv()
                    span_across(way, hop).start()

                if (way, hop + 1) in span_hops():

                    @pl.when(span_goes(way, hop + 1))
                    def _(way=way):
                        span_ring(way, hop + 1).start()

    def misc(at, src, dst, device):
        return pltpu.make_async_remote_copy(
            src_ref=src,
            dst_ref=dst,
            send_sem=misc_send.at[at],
            recv_sem=misc_recv.at[at],
            device_id=device,
            device_id_type=MESH,
        )

    q_copy = misc(0, qb.at[0], qb.at[1], other)
    kept = pl.ds(pl.multiple_of(half * 64, 64), 64)
    mine = pl.ds(span_base_of(0, 0), QROWS)
    given = pl.ds(pl.multiple_of(span_base_of(0, 0) + (1 - half) * 64, 64), 64)
    h_copy = misc(1, kv.at[given, :], hbuf.at[half], mate)
    half_rows = [pl.ds(h * 4 * QROWS, 4 * QROWS) for h in (0, 1)]
    o_copies = [
        misc(2 + h, o_send.at[half_rows[h], :], o_recv.at[half_rows[h], :], other) for h in (0, 1)
    ]
    l_copies = [misc(4 + h, l_send.at[h], l_recv.at[h], other) for h in (0, 1)]

    def run(todo):
        for what in todo:
            if what[0] == 0:
                pass_on(what[1], what[2])
            elif what[0] == 1:
                for slot in what[1]:
                    for part in (0, 1):
                        across(slot, part).wait_recv()
                    if slot == 0:
                        span_across(0, 0).wait_recv()
                    for way, hop in span_hops():
                        if SLOT_OF[way][hop] == slot:

                            @pl.when(span_comes(way, hop))
                            def _(way=way, hop=hop):
                                span_across(way, hop).wait_recv()

            elif what[0] == 2:
                q_copy.wait_recv()
            else:
                pass_span(what[1])

    left, right = pl.ds(0, HD), pl.ds(HD, HD)
    local = [
        pltpu.make_async_copy(src, dst, local_sem.at[at])
        for at, (src, dst) in enumerate(
            (
                (ctx_k, kv.at[pl.ds(0, CROWS), left]),
                (ctx_v, kv.at[pl.ds(0, CROWS), right]),
                (key_span, kv.at[mine, left]),
                (value_span, kv.at[mine, right]),
                (query, qb.at[0]),
                (dec_q.at[0], dqb),
                (cache_k.at[0], ckb),
                (cache_v.at[0], cvb),
                (key_span.at[kept, :], hbuf.at[half, :, left]),
                (value_span.at[kept, :], hbuf.at[half, :, right]),
            )
        )
    ]
    barrier = pltpu.get_barrier_semaphore()
    for device in (nxt, prv, core, other, mate):
        pl.semaphore_signal(barrier, inc=1, device_id=device, device_id_type=MESH)
    for copy in local:
        copy.start()
    for copy in local[:5]:
        copy.wait()
    pl.semaphore_wait(barrier, 5)

    for way in (0, 1):
        ring(way, 1, 0).start()
    for way in (0, 1):
        pl.when(span_goes(way, 1))(lambda way=way: span_ring(way, 1).start())
    for way in (0, 1):
        ring(way, 1, 1).start()
    for part in (0, 1):
        across(0, part).start()
    span_across(0, 0).start()
    q_copy.start()
    h_copy.start()

    row = lax.broadcasted_iota(jnp.int32, (QROWS, HD), 0)
    col = lax.broadcasted_iota(jnp.int32, (QROWS, HD), 1)
    ident[...] = jnp.where(row == col, 1.0, 0.0).astype(BF)
    limit = offset[0]
    long_row = lax.broadcasted_iota(jnp.int32, (CROWS, HD), 0)

    for slot in range(8):
        way, hop = (0, (slot + 1) // 2) if slot % 2 or slot == 0 else (1, slot // 2)
        z_slot = (z + Z - hop) % Z if way == 0 else (z + hop) % Z
        for theirs in (0, 1):
            block = z_slot * 4 + y * 2 + (c if theirs == 0 else 1 - c)
            far = pl.ds(base_of(slot, theirs), CROWS)
            near = pl.ds(span_base_of(slot, theirs), QROWS)
            long = jnp.where(long_row + block * CROWS >= limit, MASKED, 0.0).astype(BF)
            for b in (0, 1):
                y_b = y if b == 0 else 1 - y
                ahead = (block - (z * 4 + y_b * 2 + c)) * QROWS
                mask[b, far, :] = long
                mask[b, near, :] = jnp.where(row + ahead > col, MASKED, 0.0).astype(BF)

            if slot:

                @pl.when(jnp.logical_not(span_comes(way, hop)))
                def _(near=near):
                    kv[near, :] = jnp.zeros((QROWS, 2 * HD), BF)

    m_ref[...] = jnp.full_like(m_ref, M_START)
    acc_ref[...] = jnp.zeros_like(acc_ref)

    for copy in local[5:]:
        copy.wait()
    dq = dqb[...].astype(F32)
    picked = [slots[half, b] for b in range(4)]
    live = [lengths[half, b] for b in range(4)]
    place = lax.broadcasted_iota(jnp.int32, (64, 512), 1)
    request = lax.broadcasted_iota(jnp.int32, (64, 512), 0) % 8
    ok = jnp.concatenate(
        [(request == b) & (place < live[b]) for b in range(4)], axis=1
    )
    blank = jnp.zeros((4, HD), F32)
    for head in (0, 1):
        lanes = slice(head * HD, (head + 1) * HD)
        q = jnp.concatenate(
            [
                part
                for g in range(GROUPS)
                for part in (dq[:, (head * 8 + g) * HD : (head * 8 + g + 1) * HD], blank)
            ],
            axis=0,
        ).astype(BF)
        k = jnp.concatenate([ckb[picked[b]][:, lanes] for b in range(4)], axis=0)
        v = jnp.concatenate([cvb[picked[b]][:, lanes] for b in range(4)], axis=0)
        s = lax.dot_general(q, k, (((1,), (1,)), ((), ())), preferred_element_type=F32)
        s = jnp.where(ok, s * SCALE2, MASKED)
        top = jnp.max(s, axis=1, keepdims=True)
        w = jnp.where(ok, jnp.exp2(s - top), 0.0)
        total = jnp.sum(w, axis=1, keepdims=True)
        o = lax.dot_general(
            w.astype(BF), v, (((1,), (0,)), ((), ())), preferred_element_type=F32
        )
        o = o / total
        for g in range(GROUPS):
            out_dec[0, :, (head * 8 + g) * HD : (head * 8 + g + 1) * HD] = o[
                g * 8 : g * 8 + 4, :
            ].astype(BF)

    def scores_block(b, key_off, width):
        keys = pl.ds(pl.multiple_of(key_off, 256), width)
        k = jnp.concatenate([kv[keys, :HD], mask[b, keys, :]], axis=1)
        v = jnp.concatenate([kv[keys, HD:], jnp.ones((width, HD), BF)], axis=1)
        eye = jnp.concatenate([ident[...]] * 2, axis=0)
        all_s = []
        for t in range(4):
            q = jnp.concatenate(
                [qb[b, :, (2 * t + u) * HD : (2 * t + u + 1) * HD] for u in (0, 1)], axis=0
            )
            q = jnp.concatenate([q, eye], axis=1)
            all_s.append(
                lax.dot_general(q, k, (((1,), (1,)), ((), ())), preferred_element_type=F32)
            )
        for t in range(4):
            s = all_s[t]
            at = pl.ds(t * TILE, TILE)
            before = m_ref[b, at, :]
            now = jnp.maximum(before, jnp.max(s, axis=1, keepdims=True) * SCALE2)
            factor = jnp.exp2(before - now)
            p = jnp.exp2(s * SCALE2 - now[:, :1])
            m_ref[b, at, :] = now
            pv = lax.dot_general(
                p.astype(BF), v, (((1,), (0,)), ((), ())), preferred_element_type=F32
            )
            acc_ref[b, at, :] = acc_ref[b, at, :] * jnp.concatenate([factor, factor], axis=1) + pv

    def one_step(i, carry):
        for step, todo in DUTIES.items():
            pl.when(i == step)(lambda todo=todo: run(todo))
        b = pick(i, [s[0] for s in STEPS])
        off = pick(i, [s[1] for s in STEPS])
        width = pick(i, [s[2] for s in STEPS])
        spare = pick(i, [s[3] + 1 for s in STEPS])
        off = off + jnp.where(z < spare, pick(i, [s[4] for s in STEPS]), 0)
        width = jnp.where(z < spare, (width // 5) * 4, width)
        for size in (1024, 1280, 2048, 2560):
            pl.when(width == size)(lambda size=size: scores_block(b, off, size))

        @pl.when(i == SEND_AFTER)
        def _():
            eye = ident[...].astype(F32)
            for h in (0, 1):
                for g in range(4):
                    at = pl.ds((h * 4 + g) * QROWS, QROWS)
                    total = acc_ref[1, at, HD:]
                    o_send[at, :] = (acc_ref[1, at, :HD] / total).astype(BF)
                    level = m_ref[1, at, :] + jnp.log(total) * 1.4426950408889634
                    l_send[h, g : g + 1, :] = jnp.sum(level * eye, axis=0, keepdims=True)
                l_copies[h].start()
                o_copies[h].start()

        return carry

    lax.fori_loop(0, len(STEPS), one_step, 0)

    h_copy.wait()
    for u in (0, 1):
        out_hand[0, :, u * 2 * HD : (u + 1) * 2 * HD] = hbuf[u]
    for hop in (1, 2, 3, 4):
        for turn in (0, 1):
            for way in (0, 1):
                if has_hop(hop, turn):
                    ring(way, hop, turn).wait_send()
    for slot in range(8):
        for part in (0, 1):
            across(slot, part).wait_send()
    span_across(0, 0).wait_send()
    for way, hop in span_hops():
        pl.when(span_goes(way, hop))(lambda way=way, hop=hop: span_ring(way, hop).wait_send())
        pl.when(span_comes(way, hop))(lambda way=way, hop=hop: span_across(way, hop).wait_send())
    q_copy.wait_send()
    eye = ident[...].astype(F32)
    for h in (0, 1):
        l_copies[h].wait()
        o_copies[h].wait()
        for g in range(4):
            head = h * 4 + g
            at = pl.ds(head * QROWS, QROWS)
            level = jnp.sum(eye * l_recv[h, g : g + 1, :], axis=1, keepdims=True)
            mine = m_ref[0, at, :]
            top = jnp.maximum(mine, level)
            w_mine = jnp.exp2(mine - top)
            w_other = jnp.exp2(level - top)
            total = acc_ref[0, at, HD:] * w_mine + w_other
            o = acc_ref[0, at, :HD] * w_mine + o_recv[at, :].astype(F32) * w_other
            out_att[:, head * HD : (head + 1) * HD] = (o / total).astype(BF)


def deliver(a, b, c, out_a, out_b, out_c):
    out_a[...] = a[...]
    out_b[...] = b[...]
    out_c[...] = c[...]


def on_device(*args):
    anywhere = pl.BlockSpec(memory_space=pl.ANY)
    vmem = pl.BlockSpec(memory_space=pltpu.VMEM)
    smem = pl.BlockSpec(memory_space=pltpu.SMEM)
    dma = pltpu.SemaphoreType.DMA
    shapes = (
        jax.ShapeDtypeStruct((QROWS, GROUPS * HD), BF),
        jax.ShapeDtypeStruct((1, 64, 512), BF),
        jax.ShapeDtypeStruct((1, 4, 2048), BF),
    )
    results = pl.pallas_call(
        kernel,
        out_shape=shapes,
        in_specs=[
            anywhere,
            anywhere,
            anywhere,
            anywhere,
            anywhere,
            smem,
            anywhere,
            smem,
            smem,
            anywhere,
            anywhere,
        ],
        out_specs=(vmem, vmem, vmem),
        scratch_shapes=[
            pltpu.VMEM((2, QROWS, GROUPS * HD), BF),
            pltpu.VMEM((ALL_ROWS, 2 * HD), BF),
            pltpu.VMEM((2, ALL_ROWS, HD), BF),
            pltpu.VMEM((QROWS, HD), BF),
            pltpu.VMEM((2, GROUPS * QROWS, HD), F32),
            pltpu.VMEM((2, GROUPS * QROWS, 2 * HD), F32),
            pltpu.VMEM((GROUPS * QROWS, HD), BF),
            pltpu.VMEM((GROUPS * QROWS, HD), BF),
            pltpu.VMEM((2, 4, HD), F32),
            pltpu.VMEM((2, 4, HD), F32),
            pltpu.VMEM((2, 64, 2 * HD), BF),
            pltpu.VMEM((4, 2048), BF),
            pltpu.VMEM((6, 512, 256), BF),
            pltpu.VMEM((6, 512, 256), BF),
            dma((16,)),
            dma((16,)),
            dma((16,)),
            dma((16,)),
            dma((8,)),
            dma((8,)),
            dma((8,)),
            dma((8,)),
            dma((6,)),
            dma((6,)),
            dma((10,)),
        ],
        compiler_params=pltpu.CompilerParams(
            collective_id=0, has_side_effects=True, vmem_limit_bytes=56 * 2**20
        ),
        cost_estimate=pl.CostEstimate(
            flops=12 * 10**9, bytes_accessed=8 * 10**6, transcendentals=22 * 10**6
        ),
    )(*args)
    return pl.pallas_call(
        deliver,
        out_shape=shapes,
        in_specs=[vmem] * 3,
        out_specs=(vmem,) * 3,
    )(*results)


def solution(mesh):
    placed = (
        P(("seq", "rep"), "tp"),
        P(("seq", "rep"), "tp"),
        P(("seq", "rep"), "tp"),
        P(("seq", "rep"), "tp"),
        P(("seq", "rep"), "tp"),
        P(),
        P("tp", ("seq", "rep"), None),
        P(None, ("seq", "rep")),
        P(None, ("seq", "rep")),
        P("tp", ("seq", "rep"), None, None),
        P("tp", ("seq", "rep"), None, None),
    )
    return jax.shard_map(
        on_device,
        mesh=mesh,
        in_specs=placed,
        out_specs=(
            P(("seq", "rep"), "tp"),
            P("tp", ("seq", "rep"), None),
            P("tp", ("seq", "rep"), None),
        ),
        check_vma=False,
    )
```
